256 devices in a mesh: dp: 16 (over z, y_lo), land: 16 (over x, y_hi, core).
Axes of the slice: x: 4, y: 4 (y_hi: 2, y_lo: 2; y = y_hi * 2 + y_lo), z: 8, core: 2. Of those that a mesh axis runs over, the one named last changes fastest.
Arguments:
- points: bfloat16 [28672, 768], P(('dp', 'land'))
- landmarks: bfloat16 [32768, 768], P('land')
- factor: bfloat16 [32768, 1024], P('land'), may hold values from -0.03125 to 0.03125
- assignments: int32 [28672], P(('dp', 'land')), may hold values from 0 to 16383, as said below
- owner_map: int32 [16384], replicated, may hold values from 0 to 16383, as said below
- old_centroids: float32 [16384, 1024], P('dp', 'land'), may hold values from -6 to 6
Outputs:
- features: bfloat16 [28672, 1024], P(('dp', 'land'))
- centroids: float32 [16384, 1024], P('dp', 'land')
The draws below stay inside these ranges and needn't reach their ends.
Inputs may be any that keep to these rules, and one draw needn't show every extreme that they name: A permutation of 0 to 16383: cluster c has row owner_map[c] of the centroid table, and its owner is owner_map[c] // 1024. `assignments`: among the 112 points of one device, exactly 28 lie in clusters of one owner and at most 28 in clusters of any other owner. Every owner has at least one of its clusters that no point names.
All inputs are finite; a program needn't handle non-finite values.
Results may differ from the reference program's by a relative error of at most 0.0064.
Values may be sent and summed in bfloat16 or wider, within the bound.
A program may use at most 64 MiB of HBM per device.

```python
import math
import jax
import jax.numpy as jnp
from jax import lax

EMB = 768
LANDMARKS = 32768
RANK = 1024
CLUSTERS = 16384
PTS_DEV = 112
NPTS = 28672
KD = 1024
CAP = 28
N_DP = 16


def shared_table(key):
    return jax.random.permutation(jax.random.fold_in(key, 100), CLUSTERS).astype(jnp.int32)


def draw_points(key, part):
    key = jax.random.fold_in(key, 1)
    values = jax.random.normal(key, (NPTS, EMB), jnp.float32)
    return values.astype(jnp.bfloat16)


def draw_landmarks(key, part):
    key = jax.random.fold_in(key, 2)
    values = jax.random.normal(key, (LANDMARKS, EMB), jnp.float32)
    return values.astype(jnp.bfloat16)


def draw_owner_map(key, part):
    slot_table = shared_table(key)
    return slot_table


def draw_assignments(key, part):
    slot_table = shared_table(key)
    key = jax.random.fold_in(key, 4)
    inverse = jnp.argsort(slot_table, stable=True).astype(jnp.int32)
    blocks = NPTS // PTS_DEV
    key_heavy, key_others, key_jump, key_shuffle, key_local, key_skip = jax.random.split(key, 6)
    heavy_owner = jax.random.randint(key_heavy, (blocks, 1), 0, N_DP)
    other_scores = jax.random.randint(key_others, (blocks, N_DP - 1), 0, 1 << 20) * N_DP + jnp.arange(N_DP - 1, dtype=jnp.int32)[None, :]
    others_order = jnp.argsort(other_scores, axis=1, stable=True).astype(jnp.int32)
    others = (heavy_owner + 1 + others_order) % N_DP
    position_ids = jnp.arange(PTS_DEV, dtype=jnp.int32)[None, :]
    jump_bits = jax.random.randint(key_jump, (blocks, PTS_DEV), 0, 2)
    other_index = (position_ids - CAP + jump_bits) % (N_DP - 1)
    light_owner = jnp.take_along_axis(others, other_index, axis=1)
    owner_ids = jnp.where(position_ids < CAP, heavy_owner, light_owner)
    shuffle_scores = jax.random.randint(key_shuffle, (blocks, PTS_DEV), 0, 1 << 20) * PTS_DEV + position_ids
    shuffled = jnp.argsort(shuffle_scores, axis=1, stable=True).astype(jnp.int32)
    owner_ids = jnp.take_along_axis(owner_ids, shuffled, axis=1)
    skipped = jax.random.randint(key_skip, (N_DP,), 0, KD).astype(jnp.int32)
    local_ids = jax.random.randint(key_local, (blocks, PTS_DEV), 0, KD - 1).astype(jnp.int32)
    local_ids = local_ids + (local_ids >= jnp.take(skipped, owner_ids)).astype(jnp.int32)
    slot_ids = owner_ids * KD + local_ids
    return jnp.take(inverse, slot_ids.reshape(NPTS)).astype(jnp.int32)


def steps_of(rng, shape, cuts, smallest, high):
    def one(dim, blocks):
        steps = jax.random.uniform(jax.random.fold_in(jax.random.fold_in(rng, 6), dim), (blocks,), jnp.float32, smallest / len(cuts), high / len(cuts))
        return jnp.repeat(jnp.exp(steps), shape[dim] // blocks).reshape((-1,) + (1,) * (len(shape) - dim - 1))

    loudness = one(*cuts[0])
    for cut in cuts[1:]:
        loudness = loudness * one(*cut)
    return loudness


def scatter_about(rng, shape, width, limit, shards=(), kind=jnp.bfloat16):
    loudness = steps_of(rng, shape, shards, -0.22, 0.18) if shards else 1.0
    result = jax.random.normal(rng, shape, jnp.float32) * width * loudness
    return jnp.minimum(jnp.maximum(result, -limit), limit).astype(kind)


def setup_inputs(seed: int = 0) -> dict:
    keys = jax.random.split(jax.random.key(seed), 7)
    points = draw_points(jax.random.fold_in(keys[6], 71), 0)
    landmarks = draw_landmarks(jax.random.fold_in(keys[6], 71), 0)
    factor = scatter_about(keys[2], (LANDMARKS, RANK), LANDMARKS ** -0.5, 0.03125, ((0, 16),))
    assignments = draw_assignments(jax.random.fold_in(keys[6], 71), 0)
    owner_map = draw_owner_map(jax.random.fold_in(keys[6], 71), 0)
    old_centroids = scatter_about(keys[5], (CLUSTERS, RANK), 1.0, 6.0, ((0, 16), (1, 16)), jnp.float32)
    return {"points": points, "landmarks": landmarks, "factor": factor, "assignments": assignments, "owner_map": owner_map, "old_centroids": old_centroids}


def unit_rows(values):
    widened = values.astype(jnp.float32)
    squared_sum = lax.optimization_barrier(jnp.sum(widened * widened, axis=1, keepdims=True)) + 1e-06
    return (widened * lax.rsqrt(squared_sum)).astype(jnp.bfloat16)

def kernel_block(shard_rows, unit_land, sharpness):
    scores = lax.dot_general(shard_rows, unit_land, (((1,), (1,)), ((), ())), preferred_element_type=jnp.float32)
    return jnp.exp(sharpness * scores).astype(jnp.bfloat16)

def reference(points, landmarks, factor, assignments, owner_map, old_centroids):
    sharpness = math.sqrt(EMB)
    unit_land = unit_rows(landmarks)
    blocks = unit_rows(points).reshape(NPTS // PTS_DEV, PTS_DEV, EMB)

    def one_block(shard_rows):
        kernel_rows = kernel_block(shard_rows, unit_land, sharpness)
        return jnp.dot(kernel_rows, factor, preferred_element_type=jnp.float32).astype(jnp.bfloat16)
    features = lax.map(one_block, blocks).reshape(NPTS, RANK)
    slot_ids = jnp.take(owner_map, assignments).astype(jnp.int32)
    totals = jax.ops.segment_sum(features.astype(jnp.float32), slot_ids, num_segments=CLUSTERS)
    counts = jax.ops.segment_sum(jnp.ones((NPTS,), jnp.float32), slot_ids, num_segments=CLUSTERS)
    centroids = jnp.where(counts[:, None] > 0, totals / jnp.maximum(counts, 1.0)[:, None], old_centroids)
    return (features, centroids)
```

```python
import functools
import math

import jax
import jax.numpy as jnp
from jax import lax
from jax.experimental import pallas as pl
from jax.experimental.pallas import tpu as pltpu
from jax.sharding import PartitionSpec as P

MESH = pl.DeviceIdType.MESH
F32 = jnp.float32
BF16 = jnp.bfloat16

EMB = 768
RANK = 1024
PTS = 112
SRC = 8
OWN = 16
KD = 1024
ROWS = (32, 32, 32, 16)
CAPS = (8, 8, 8, 4)
STARTS = (0, 32, 64, 96)
CHUNKS = 4
TILE = 1024
LM = 2048
COLS = 128
NT = (((1,), (1,)), ((), ()))


def unit_rows(values):
    widened = values.astype(F32)
    squared_sum = jnp.sum(widened * widened, axis=1, keepdims=True) + 1e-06
    return (widened * lax.rsqrt(squared_sum)).astype(BF16)


def body(
    sharpness,
    points_ref,
    perm_ref,
    back_ref,
    meta_ref,
    land_ref,
    factor_ref,
    old_ref,
    feat_ref,
    cent_ref,
    land,
    fac,
    metas,
    sorted_pts,
    featq,
    counts,
    pcounts,
    totals,
    flipped,
    ptotals,
    lab_send,
    lab_recv,
    ag,
    acc,
    ppart,
    rs_send,
    rs_recv,
    poh,
    oh,
    dp_send,
    dp_recv,
    local_sem,
    meta_sems,
    ag_sems,
    fwd_sems,
    pair_sems,
    rs_sems,
    back_sems,
    lab_sems,
    dp_sems,
    fin_sems,
):
    dp = lax.axis_index("dp")
    la = lax.axis_index("land")
    me = la // 2
    core = la % 2
    ylo = dp % 2
    z = dp // 2

    def chip(delta):
        other = (me + delta) % SRC
        lo = (ylo + me % 2 + other % 2) % 2
        return {"dp": z * 2 + lo, "land": other * 2 + core}

    def owner(delta):
        return {"dp": (dp + delta) % OWN, "land": la}

    partner = {"dp": dp, "land": me * 2 + 1 - core}

    def send(src, dst, sems, slot, device):
        return pltpu.make_async_remote_copy(
            src_ref=src,
            dst_ref=dst,
            send_sem=sems.at[(0,) + slot],
            recv_sem=sems.at[(1,) + slot],
            device_id=device,
            device_id_type=MESH,
        )

    def meta_copy(delta):
        return send(meta_ref, metas.at[delta], meta_sems, (delta,), chip(delta))

    def ag_copy(k, delta):
        n = ROWS[k]
        return send(
            sorted_pts.at[pl.ds(STARTS[k], n), :],
            ag[k].at[pl.ds(pl.multiple_of(me * n, n), n), :],
            ag_sems,
            (k, delta),
            chip(delta),
        )

    def fwd_copy(k):
        n = ROWS[k] * SRC
        return send(ag[k].at[pl.ds(0, n), :], ag[k].at[pl.ds(n, n), :], fwd_sems, (k,), partner)

    def pair_copy(k):
        n = ROWS[k] * SRC
        return send(acc[k].at[pl.ds(n, n), :], ppart[k], pair_sems, (k,), partner)

    def rs_copy(k, delta):
        return send(rs_send[k].at[delta], rs_recv[k].at[delta], rs_sems, (k, delta), chip(delta))

    def back_copy(k, delta):
        n = ROWS[k]
        other = (me + delta) % SRC
        return send(
            dp_recv_feat(k).at[pl.ds(pl.multiple_of(other * n, n), n), :],
            featq.at[pl.ds(STARTS[k], n), pl.ds(pl.multiple_of(me * COLS, COLS), COLS)],
            back_sems,
            (k, delta),
            chip(delta),
        )

    def dp_recv_feat(k):
        return rs_recv[k].at[0]

    def lab_copy(delta):
        return send(
            lab_send.at[(dp + delta) % OWN], lab_recv.at[dp], lab_sems, (delta,), owner(delta)
        )

    def dp_copy(k, delta):
        n = SRC * CAPS[k]
        to = (dp + delta) % OWN
        return send(
            dp_send[k].at[pl.ds(pl.multiple_of(to * n, n), n), :],
            dp_recv[k].at[pl.ds(pl.multiple_of(dp * n, n), n), :],
            dp_sems,
            (k, delta),
            owner(delta),
        )

    def count_copy():
        return send(counts, pcounts, fin_sems, (0,), partner)

    def total_copy():
        half = pl.ds(pl.multiple_of((1 - core) * 64, 64), 64)
        return send(flipped.at[half, :], ptotals, fin_sems, (1,), partner)

    barrier = pltpu.get_barrier_semaphore()
    pl.semaphore_signal(barrier, inc=1, device_id=partner, device_id_type=MESH)
    for delta in range(1, SRC):
        pl.semaphore_signal(barrier, inc=1, device_id=chip(delta), device_id_type=MESH)
    for delta in range(1, OWN):
        pl.semaphore_signal(barrier, inc=1, device_id=owner(delta), device_id_type=MESH)
    load_land = pltpu.make_async_copy(land_ref, land, local_sem.at[0])
    load_fac = pltpu.make_async_copy(factor_ref, fac, local_sem.at[1])
    load_land.start()
    load_fac.start()

    unit_points = unit_rows(points_ref[...])
    sorted_pts[...] = jnp.dot(perm_ref[...], unit_points, preferred_element_type=F32).astype(BF16)
    for k in range(CHUNKS):
        n = ROWS[k]
        ag[k][pl.ds(pl.multiple_of(me * n, n), n), :] = sorted_pts[STARTS[k] : STARTS[k] + n, :]

    pl.semaphore_wait(barrier, SRC + OWN - 1)

    for delta in range(1, SRC):
        ag_copy(0, delta).start()
    for delta in range(1, SRC):
        meta_copy(delta).start()
    for k in range(1, CHUNKS):
        for delta in range(1, SRC):
            ag_copy(k, delta).start()

    load_land.wait()

    @pl.loop(0, LM // 256)
    def _(t):
        rows = pl.ds(pl.multiple_of(t * 256, 256), 256)
        land[rows, :] = unit_rows(land[rows, :])

    load_fac.wait()

    def gather_chunk(k):
        for delta in range(1, SRC):
            ag_copy(k, delta).wait_recv()
        fwd_copy(k).start()

    scale = sharpness * math.log2(math.e)

    def matmul(k, part):
        n = ROWS[k] * SRC
        mine = pl.ds(part * n, n)
        for t in range(LM // TILE):
            rows = pl.ds(t * TILE, TILE)
            scores = lax.dot_general(ag[k][mine, :], land[rows, :], NT, preferred_element_type=F32)
            kernel = jnp.exp2(scores * scale).astype(BF16)
            share = jnp.dot(kernel, fac[rows, :], preferred_element_type=F32)
            if t == 0:
                acc[k][mine, :] = share
            else:
                acc[k][mine, :] += share

    def labels():
        for delta in range(1, SRC):
            meta_copy(delta).wait_recv()
        merged = meta_ref[...]
        for delta in range(1, SRC):
            merged = merged + metas[delta]
        owners_col = lax.broadcasted_iota(jnp.int32, (OWN, 256), 0)
        lane_col = lax.broadcasted_iota(jnp.int32, (COLS, 256), 0)
        found = []
        for k in range(CHUNKS):
            n = SRC * CAPS[k]
            pts = ROWS[k] * SRC
            code = merged[k : k + 1, :pts] - 1
            local = merged[CHUNKS + k : CHUNKS + k + 1, :pts]
            slot = lax.broadcasted_iota(jnp.int32, (OWN * n, pts), 0)
            poh[k][...] = jnp.where(slot == code, 1.0, 0.0).astype(BF16)
            to = code // n
            lane = code - to * n + (dp % (COLS // n)) * n
            hit = owners_col[:, :pts] == to
            high = jnp.where(hit, local // 32, 0).astype(F32).astype(BF16)
            low = jnp.where(hit, local % 32, 0).astype(F32).astype(BF16)
            place = jnp.where(lane_col[:, :pts] == lane, 1.0, 0.0).astype(BF16)
            high = lax.dot_general(high, place, NT, preferred_element_type=F32)
            low = lax.dot_general(low, place, NT, preferred_element_type=F32)
            found.append((high * 32.0 + low).astype(jnp.int32))
        for o in range(OWN):
            for k in range(CHUNKS):
                lab_send[o, :, k * COLS : (k + 1) * COLS] = found[k][o : o + 1, :]
        for delta in range(1, OWN):
            lab_copy(delta).start()
        lab_recv[dp] = lab_send[dp]

    def hits():
        for delta in range(1, OWN):
            lab_copy(delta).wait_recv()
        cluster = lax.broadcasted_iota(jnp.int32, (KD, COLS), 0) + 1
        for k in range(CHUNKS):
            share = COLS // (SRC * CAPS[k])
            for m in range(OWN // share):
                label = lab_recv[m * share][:, k * COLS : (k + 1) * COLS]
                for i in range(1, share):
                    label = label + lab_recv[m * share + i][:, k * COLS : (k + 1) * COLS]
                hit = jnp.where(cluster == label, 1.0, 0.0).astype(BF16)
                oh[k][:, m * COLS : (m + 1) * COLS] = hit
        ones = jnp.ones((OWN * SRC * CAPS[0], COLS), BF16)
        total = jnp.dot(oh[0][...], ones, preferred_element_type=F32)
        for k in range(1, CHUNKS):
            total += jnp.dot(oh[k][...], ones[: OWN * SRC * CAPS[k]], preferred_element_type=F32)
        counts[...] = total
        count_copy().start()

    def scatter(k):
        n = ROWS[k] * SRC
        pair_copy(k).wait_recv()
        for delta in range(1, SRC):
            other = pl.ds(pl.multiple_of((me + delta) % SRC * COLS, COLS), COLS)
            both = acc[k][pl.ds(0, n), other] + ppart[k][:, other]
            rs_send[k][delta] = both.astype(BF16)
            rs_copy(k, delta).start()

    def reduce_rows(k):
        n = ROWS[k]
        here = pl.ds(pl.multiple_of(me * COLS, COLS), COLS)
        rows = acc[k][pl.ds(0, n * SRC), here] + ppart[k][:, here]
        for delta in range(1, SRC):
            rs_copy(k, delta).wait_recv()
            rows = rows + rs_recv[k][delta].astype(F32)
        rows = rows.astype(BF16)
        packed = jnp.dot(poh[k][...], rows, preferred_element_type=F32)
        dp_send[k][...] = packed.astype(BF16)
        for delta in range(1, OWN):
            dp_copy(k, delta).start()
        m = SRC * CAPS[k]
        mine = pl.ds(pl.multiple_of(dp * m, m), m)
        dp_recv[k][mine, :] = dp_send[k][mine, :]
        rs_recv[k][0] = rows
        for delta in range(1, SRC):
            back_copy(k, delta).start()
        featq[STARTS[k] : STARTS[k] + n, here] = rs_recv[k][
            0, pl.ds(pl.multiple_of(me * n, n), n), :
        ]

    def add_owned(k):
        for delta in range(1, OWN):
            dp_copy(k, delta).wait_recv()
        total = jnp.dot(oh[k][...], dp_recv[k][...], preferred_element_type=F32)
        if k == 0:
            totals[...] = total
        else:
            totals[...] += total

    gather_chunk(0)
    matmul(0, 0)
    fwd_copy(0).wait_recv()
    gather_chunk(1)
    matmul(0, 1)
    pair_copy(0).start()
    labels()
    for k in range(1, CHUNKS):
        fwd_copy(k).wait_recv()
        matmul(k, 1)
        pair_copy(k).start()
        scatter(k - 1)
        if k + 1 < CHUNKS:
            gather_chunk(k + 1)
        matmul(k, 0)
        if k == 1:
            hits()
        if k >= 2:
            reduce_rows(k - 2)
        if k >= 3:
            add_owned(k - 3)
    scatter(CHUNKS - 1)
    reduce_rows(CHUNKS - 2)
    add_owned(CHUNKS - 3)
    reduce_rows(CHUNKS - 1)
    add_owned(CHUNKS - 2)
    for k in range(CHUNKS):
        for delta in range(1, SRC):
            back_copy(k, delta).wait_recv()
    feat_ref[...] = jnp.dot(back_ref[...], featq[...], preferred_element_type=F32).astype(BF16)
    count_copy().wait_recv()
    add_owned(CHUNKS - 1)

    flipped[...] = totals[...].T
    total_copy().start()
    seen = (counts[...] + pcounts[...]).T[:64]
    safe = jnp.maximum(seen, 1.0)
    old = old_ref[...]
    total_copy().wait_recv()
    mine = flipped[pl.ds(pl.multiple_of(core * 64, 64), 64), :] + ptotals[...]
    cent_ref[...] = jnp.where(seen > 0, mine / safe, old)

    for delta in range(1, SRC):
        meta_copy(delta).wait_send()
    for delta in range(1, OWN):
        lab_copy(delta).wait_send()
    for k in range(CHUNKS):
        fwd_copy(k).wait_send()
        pair_copy(k).wait_send()
        for delta in range(1, SRC):
            ag_copy(k, delta).wait_send()
            rs_copy(k, delta).wait_send()
            back_copy(k, delta).wait_send()
        for delta in range(1, OWN):
            dp_copy(k, delta).wait_send()
    count_copy().wait_send()
    total_copy().wait_send()


def per_device(points, landmarks, factor, assignments, owner_map, old_centroids):
    sharpness = math.sqrt(points.shape[1])
    chip = lax.axis_index("land") // 2
    slot_ids = jnp.take(owner_map, assignments)
    owner_ids = slot_ids // KD
    local_ids = slot_ids % KD
    hits = (owner_ids[:, None] == jnp.arange(OWN, dtype=jnp.int32)[None, :]).astype(jnp.int32)
    before = jnp.cumsum(hits, axis=0) - hits
    rank = jnp.sum(before * hits, axis=1)
    smaller = jnp.sum((owner_ids[None, :] < owner_ids[:, None]).astype(jnp.int32), axis=1)
    place = smaller + rank
    part = place % 7
    index = part * 16 + place // 7
    turn = rank // 7
    chunk = part // 2
    last = chunk == 3
    step = jnp.where(last, turn, (part % 2) * 4 + turn)
    cap = jnp.where(last, 4, 8)
    code = owner_ids * (SRC * cap) + chip * cap + step
    lane = chip * jnp.where(last, 16, 32) + index - chunk * 32
    perm = jnp.arange(PTS, dtype=jnp.int32)[:, None] == index[None, :]
    back = index[:, None] == jnp.arange(PTS, dtype=jnp.int32)[None, :]
    rows = jnp.arange(8, dtype=jnp.int32)[:, None, None]
    lanes = jnp.arange(256, dtype=jnp.int32)[None, :, None]
    values = jnp.where(rows < 4, code + 1, local_ids + 1)
    meta = jnp.sum(jnp.where((rows % 4 == chunk) & (lanes == lane), values, 0), axis=2)

    vmem = pl.BlockSpec(memory_space=pltpu.VMEM)
    hbm = pl.BlockSpec(memory_space=pl.ANY)
    chunks = range(CHUNKS)
    features, centroids = pl.pallas_call(
        functools.partial(body, sharpness),
        out_shape=(
            jax.ShapeDtypeStruct((PTS, RANK), BF16),
            jax.ShapeDtypeStruct((64, KD), F32),
        ),
        in_specs=[vmem, vmem, vmem, vmem, hbm, hbm, vmem],
        out_specs=(vmem, vmem),
        scratch_shapes=[
            pltpu.VMEM((LM, EMB), BF16),
            pltpu.VMEM((LM, RANK), BF16),
            pltpu.VMEM((SRC, 8, 256), jnp.int32),
            pltpu.VMEM((PTS, EMB), BF16),
            pltpu.VMEM((PTS, RANK), BF16),
            pltpu.VMEM((KD, COLS), F32),
            pltpu.VMEM((KD, COLS), F32),
            pltpu.VMEM((KD, COLS), F32),
            pltpu.VMEM((COLS, KD), F32),
            pltpu.VMEM((64, KD), F32),
            pltpu.VMEM((OWN, 1, CHUNKS * COLS), jnp.int32),
            pltpu.VMEM((OWN, 1, CHUNKS * COLS), jnp.int32),
            [pltpu.VMEM((2 * SRC * ROWS[k], EMB), BF16) for k in chunks],
            [pltpu.VMEM((2 * SRC * ROWS[k], RANK), F32) for k in chunks],
            [pltpu.VMEM((SRC * ROWS[k], RANK), F32) for k in chunks],
            [pltpu.VMEM((SRC, SRC * ROWS[k], COLS), BF16) for k in chunks],
            [pltpu.VMEM((SRC, SRC * ROWS[k], COLS), BF16) for k in chunks],
            [pltpu.VMEM((OWN * SRC * CAPS[k], SRC * ROWS[k]), BF16) for k in chunks],
            [pltpu.VMEM((KD, OWN * SRC * CAPS[k]), BF16) for k in chunks],
            [pltpu.VMEM((OWN * SRC * CAPS[k], COLS), BF16) for k in chunks],
            [pltpu.VMEM((OWN * SRC * CAPS[k], COLS), BF16) for k in chunks],
            pltpu.SemaphoreType.DMA((2,)),
            pltpu.SemaphoreType.DMA((2, SRC)),
            pltpu.SemaphoreType.DMA((2, CHUNKS, SRC)),
            pltpu.SemaphoreType.DMA((2, CHUNKS)),
            pltpu.SemaphoreType.DMA((2, CHUNKS)),
            pltpu.SemaphoreType.DMA((2, CHUNKS, SRC)),
            pltpu.SemaphoreType.DMA((2, CHUNKS, SRC)),
            pltpu.SemaphoreType.DMA((2, OWN)),
            pltpu.SemaphoreType.DMA((2, CHUNKS, OWN)),
            pltpu.SemaphoreType.DMA((2, 2)),
        ],
        name="nystrom",
        compiler_params=pltpu.CompilerParams(
            collective_id=1, has_side_effects=True, vmem_limit_bytes=60 * 2**20
        ),
    )(
        points,
        perm.astype(BF16),
        back.astype(BF16),
        meta,
        landmarks,
        factor,
        old_centroids.T,
    )
    return (features, centroids.T)


def solution(mesh):
    in_specs = (
        P(("dp", "land"), None),
        P("land", None),
        P("land", None),
        P(("dp", "land")),
        P(),
        P("dp", "land"),
    )
    out_specs = (P(("dp", "land"), None), P("dp", "land"))
    return jax.shard_map(
        per_device, mesh=mesh, in_specs=in_specs, out_specs=out_specs, check_vma=False
    )
```

```python
import functools
import math

import jax
import jax.numpy as jnp
from jax import lax
from jax.experimental import pallas as pl
from jax.experimental.pallas import tpu as pltpu
from jax.sharding import PartitionSpec as P

MESH = pl.DeviceIdType.MESH
F32 = jnp.float32
BF16 = jnp.bfloat16

EMB = 768
RANK = 1024
PTS = 112
SRC = 8
OWN = 16
KD = 1024
ROWS = (32, 32, 32, 16)
CAPS = (8, 8, 8, 4)
STARTS = (0, 32, 64, 96)
CHUNKS = 4
TILE = 1024
LM = 2048
COLS = 128
NT = (((1,), (1,)), ((), ()))


def unit_rows(values):
    widened = values.astype(F32)
    squared_sum = jnp.sum(widened * widened, axis=1, keepdims=True) + 1e-06
    return (widened * lax.rsqrt(squared_sum)).astype(BF16)


def body(
    sharpness,
    points_ref,
    assign_ref,
    table_ref,
    land_ref,
    factor_ref,
    featq,
    back_ref,
    sums_ref,
    seen_ref,
    land,
    fac,
    meta,
    metas,
    sorted_pts,
    counts,
    pcounts,
    totals,
    flipped,
    ptotals,
    lab_send,
    lab_recv,
    ag,
    acc,
    ppart,
    rs_send,
    rs_recv,
    poh,
    oh,
    dp_send,
    dp_recv,
    local_sem,
    meta_sems,
    ag_sems,
    fwd_sems,
    pair_sems,
    rs_sems,
    back_sems,
    lab_sems,
    dp_sems,
    fin_sems,
):
    dp = lax.axis_index("dp")
    la = lax.axis_index("land")
    me = la // 2
    core = la % 2
    ylo = dp % 2
    z = dp // 2

    def mirror(chip):
        return chip + 1 - 2 * (chip % 2)

    right = (me + 2) % SRC
    left = (me + 6) % SRC
    far = (me + 4) % SRC
    near = mirror(me)

    def device(chip):
        lo = (ylo + me % 2 + chip % 2) % 2
        return {"dp": z * 2 + lo, "land": chip * 2 + core}

    def owner(delta):
        return {"dp": (dp + delta) % OWN, "land": la}

    partner = {"dp": dp, "land": me * 2 + 1 - core}

    def send(src, dst, sems, slot, to):
        return pltpu.make_async_remote_copy(
            src_ref=src,
            dst_ref=dst,
            send_sem=sems.at[(0,) + slot],
            recv_sem=sems.at[(1,) + slot],
            device_id=to,
            device_id_type=MESH,
        )

    def at(index, size):
        return pl.ds(pl.multiple_of(index * size, size), size)

    def meta_copy(delta):
        return send(meta, metas.at[delta], meta_sems, (delta,), device((me + delta) % SRC))

    ag_steps = ((me, near), (me, right), (me, left), (me, far), (near, right), (near, left), (far, near))

    def ag_copy(k, step):
        block, to = ag_steps[step]
        n = ROWS[k]
        src = sorted_pts.at[pl.ds(STARTS[k], n), :] if step < 4 else ag[k].at[at(block, n), :]
        return send(src, ag[k].at[at(block, n), :], ag_sems, (k, step), device(to))

    def fwd_copy(k):
        n = ROWS[k] * SRC
        return send(ag[k].at[pl.ds(0, n), :], ag[k].at[pl.ds(n, n), :], fwd_sems, (k,), partner)

    def pair_copy(k):
        n = ROWS[k] * SRC
        return send(acc[k].at[pl.ds(n, n), :], ppart[k], pair_sems, (k,), partner)

    rs_steps = (
        (right, mirror(right)),
        (left, mirror(left)),
        (near, mirror(far)),
        (right, right),
        (left, left),
        (far, far),
        (near, near),
    )

    def rs_copy(k, step):
        if k == CHUNKS - 1:
            to = (me + step + 1) % SRC
        else:
            to = rs_steps[step][0]
        return send(rs_send[k].at[step], rs_recv[k].at[step], rs_sems, (k, step), device(to))

    def back_copy(k, delta):
        other = (me + delta) % SRC
        return send(
            rs_recv[k].at[7].at[at(other, ROWS[k]), :],
            featq.at[pl.ds(STARTS[k], ROWS[k]), at(me, COLS)],
            back_sems,
            (k, delta),
            device(other),
        )

    def lab_copy(delta):
        return send(
            lab_send.at[(dp + delta) % OWN], lab_recv.at[dp], lab_sems, (delta,), owner(delta)
        )

    def dp_copy(k, delta):
        n = SRC * CAPS[k]
        return send(
            dp_send[k].at[at((dp + delta) % OWN, n), :],
            dp_recv[k].at[at(dp, n), :],
            dp_sems,
            (k, delta),
            owner(delta),
        )

    def count_copy():
        return send(counts, pcounts, fin_sems, (0,), partner)

    def total_copy():
        return send(flipped.at[at(1 - core, 64), :], ptotals, fin_sems, (1,), partner)

    barrier = pltpu.get_barrier_semaphore()
    pl.semaphore_signal(barrier, inc=1, device_id=partner, device_id_type=MESH)
    for delta in range(1, SRC):
        pl.semaphore_signal(
            barrier, inc=1, device_id=device((me + delta) % SRC), device_id_type=MESH
        )
    for delta in range(1, OWN):
        pl.semaphore_signal(barrier, inc=1, device_id=owner(delta), device_id_type=MESH)
    load_land = pltpu.make_async_copy(land_ref, land, local_sem.at[0])
    load_fac = pltpu.make_async_copy(factor_ref, fac, local_sem.at[1])
    load_land.start()
    load_fac.start()

    def iota(rows, lanes):
        return lax.broadcasted_iota(jnp.int32, (rows, lanes), 0)

    def one_hot(cond):
        return jnp.where(cond, 1.0, 0.0).astype(BF16)

    def small(values):
        return values.astype(F32).astype(BF16)

    assign = assign_ref[...]
    table = table_ref[...]
    picked = one_hot(iota(128, PTS) == assign // 128)
    lane_hit = iota(128, PTS) == assign % 128

    def look_up(values):
        rows = jnp.dot(small(values.T), picked, preferred_element_type=F32)
        return jnp.sum(jnp.where(lane_hit, rows, 0.0), axis=0, keepdims=True).astype(jnp.int32)

    owner_ids = look_up(table // KD)
    high_ids = look_up(table % KD // 32)
    low_ids = look_up(table % 32)
    hits_of = iota(OWN, PTS) == owner_ids
    earlier = one_hot(iota(PTS, PTS) < lax.broadcasted_iota(jnp.int32, (PTS, PTS), 1))
    before = jnp.dot(one_hot(hits_of), earlier, preferred_element_type=F32)
    rank = jnp.sum(jnp.where(hits_of, before, 0.0), axis=0, keepdims=True).astype(jnp.int32)
    sizes = jnp.sum(jnp.where(hits_of, 1.0, 0.0), axis=1, keepdims=True)
    smaller = jnp.sum(
        jnp.where(iota(OWN, PTS) < owner_ids, sizes, 0.0), axis=0, keepdims=True
    ).astype(jnp.int32)
    place = smaller + rank
    part = place % 7
    index = part * 16 + place // 7
    perm = one_hot(iota(PTS, PTS) == index)
    sorted_pts[...] = jnp.dot(
        perm, unit_rows(points_ref[...]), preferred_element_type=F32
    ).astype(BF16)
    back_ref[...] = perm
    turn = rank // 7
    chunk = part // 2
    last = chunk == CHUNKS - 1
    step = jnp.where(last, turn, part % 2 * 4 + turn)
    cap = jnp.where(last, CAPS[3], CAPS[0])
    code = owner_ids * (SRC * cap) + me * cap + step + 1
    lane = me * jnp.where(last, ROWS[3], ROWS[0]) + index - chunk * 32
    placed = one_hot(iota(256, PTS) == lane)
    mine = iota(CHUNKS, PTS) == chunk

    def spread(values):
        return lax.dot_general(
            small(jnp.where(mine, values, 0)), placed, NT, preferred_element_type=F32
        )

    labels_of = high_ids * 32 + low_ids + 1
    meta[0:4, :] = (spread(code // 32) * 32.0 + spread(code % 32)).astype(jnp.int32)
    meta[4:8, :] = (spread(labels_of // 32) * 32.0 + spread(labels_of % 32)).astype(jnp.int32)
    for k in range(CHUNKS):
        ag[k][at(me, ROWS[k]), :] = sorted_pts[STARTS[k] : STARTS[k] + ROWS[k], :]

    pl.semaphore_wait(barrier, SRC + OWN - 1)

    def ag_own(k):
        for i in range(4):
            ag_copy(k, i).start()

    def ag_forward(k):
        ag_copy(k, 0).wait_recv()
        ag_copy(k, 4).start()
        ag_copy(k, 5).start()
        ag_copy(k, 3).wait_recv()
        ag_copy(k, 6).start()
        if k + 2 < CHUNKS:
            ag_own(k + 2)

    def gather(k):
        for i in (1, 2, 4, 5, 6):
            ag_copy(k, i).wait_recv()
        fwd_copy(k).start()

    def normalize(first, last):
        @pl.loop(first, last)
        def _(t):
            rows = at(t, 256)
            land[rows, :] = unit_rows(land[rows, :])

    scale = sharpness * math.log2(math.e)

    def matmul(k, part):
        n = ROWS[k] * SRC
        mine = pl.ds(part * n, n) if part < 2 else pl.ds(0, 2 * n)
        for t in range(LM // TILE):
            rows = pl.ds(t * TILE, TILE)
            scores = lax.dot_general(ag[k][mine, :], land[rows, :], NT, preferred_element_type=F32)
            kernel = jnp.exp2(scores * scale).astype(BF16)
            share = jnp.dot(kernel, fac[rows, :], preferred_element_type=F32)
            if t == 0:
                acc[k][mine, :] = share
            else:
                acc[k][mine, :] += share

    def labels():
        for delta in range(1, SRC):
            meta_copy(delta).wait_recv()
        merged = meta[...]
        for delta in range(1, SRC):
            merged = merged + metas[delta]
        found = []
        for k in range(CHUNKS):
            n = SRC * CAPS[k]
            pts = ROWS[k] * SRC
            code = merged[k : k + 1, :pts] - 1
            local = merged[CHUNKS + k : CHUNKS + k + 1, :pts]
            poh[k][...] = one_hot(iota(OWN * n, pts) == code)
            to = code // n
            lane = code - to * n + (dp % (COLS // n)) * n
            hit = iota(OWN, pts) == to
            place = one_hot(iota(COLS, pts) == lane)
            high = small(jnp.where(hit, local // 32, 0))
            low = small(jnp.where(hit, local % 32, 0))
            high = lax.dot_general(high, place, NT, preferred_element_type=F32)
            low = lax.dot_general(low, place, NT, preferred_element_type=F32)
            found.append((high * 32.0 + low).astype(jnp.int32))
        for o in range(OWN):
            for k in range(CHUNKS):
                lab_send[o, :, k * COLS : (k + 1) * COLS] = found[k][o : o + 1, :]
        for delta in range(1, OWN):
            lab_copy(delta).start()
        lab_recv[dp] = lab_send[dp]

    def labels_arrived():
        for delta in range(1, OWN):
            lab_copy(delta).wait_recv()

    def hits(k):
        cluster = iota(KD, COLS) + 1
        share = COLS // (SRC * CAPS[k])
        for m in range(OWN // share):
            label = lab_recv[m * share][:, k * COLS : (k + 1) * COLS]
            for i in range(1, share):
                label = label + lab_recv[m * share + i][:, k * COLS : (k + 1) * COLS]
            oh[k][:, m * COLS : (m + 1) * COLS] = one_hot(cluster == label)
        ones = jnp.ones((OWN * SRC * CAPS[k], COLS), BF16)
        total = jnp.dot(oh[k][...], ones, preferred_element_type=F32)
        if k == 0:
            counts[...] = total
        else:
            counts[...] += total
        if k == CHUNKS - 1:
            count_copy().start()

    def both(k, chip):
        n = ROWS[k] * SRC
        cols = at(chip, COLS)
        return acc[k][pl.ds(0, n), cols] + ppart[k][:, cols]

    def scatter(k):
        pair_copy(k).wait_recv()
        for i in range(5):
            rs_send[k][i] = both(k, rs_steps[i][1]).astype(BF16)
            rs_copy(k, i).start()

    def scatter_sums(k):
        rs_copy(k, 2).wait_recv()
        rs_send[k][5] = (both(k, far) + rs_recv[k][2].astype(F32)).astype(BF16)
        rs_copy(k, 5).start()
        rs_copy(k, 0).wait_recv()
        rs_copy(k, 1).wait_recv()
        joined = both(k, near) + rs_recv[k][0].astype(F32) + rs_recv[k][1].astype(F32)
        rs_send[k][6] = joined.astype(BF16)
        rs_copy(k, 6).start()

    def scatter_last(k):
        pair_copy(k).wait_recv()
        for i in range(SRC - 1):
            rs_send[k][i] = both(k, (me + i + 1) % SRC).astype(BF16)
            rs_copy(k, i).start()

    def reduce_rows(k):
        n = ROWS[k]
        rows = both(k, me)
        for i in range(0 if k == CHUNKS - 1 else 3, 7):
            rs_copy(k, i).wait_recv()
            rows = rows + rs_recv[k][i].astype(F32)
        rows = rows.astype(BF16)
        packed = jnp.dot(poh[k][...], rows, preferred_element_type=F32)
        dp_send[k][...] = packed.astype(BF16)
        for delta in range(1, OWN):
            dp_copy(k, delta).start()
        m = SRC * CAPS[k]
        dp_recv[k][at(dp, m), :] = dp_send[k][at(dp, m), :]
        rs_recv[k][7] = rows
        for delta in range(1, SRC):
            back_copy(k, delta).start()
        featq[STARTS[k] : STARTS[k] + n, at(me, COLS)] = rs_recv[k][7, at(me, n), :]

    def add_owned(k):
        for delta in range(1, OWN):
            dp_copy(k, delta).wait_recv()
        total = jnp.dot(oh[k][...], dp_recv[k][...], preferred_element_type=F32)
        if k == 0:
            totals[...] = total
        else:
            totals[...] += total

    for delta in range(1, SRC):
        meta_copy(delta).start()
    ag_own(0)
    ag_own(1)
    load_land.wait()
    normalize(0, 4)
    ag_forward(0)
    normalize(4, 8)
    labels()
    load_fac.wait()
    gather(0)
    matmul(0, 0)
    ag_forward(1)
    fwd_copy(0).wait_recv()
    matmul(0, 1)
    pair_copy(0).start()
    gather(1)
    ag_forward(2)
    labels_arrived()
    hits(0)

    fwd_copy(1).wait_recv()
    matmul(1, 1)
    pair_copy(1).start()
    scatter(0)
    ag_forward(3)
    gather(2)
    matmul(1, 0)
    scatter_sums(0)

    fwd_copy(2).wait_recv()
    matmul(2, 1)
    pair_copy(2).start()
    scatter(1)
    gather(3)
    matmul(2, 0)
    scatter_sums(1)
    reduce_rows(0)

    fwd_copy(3).wait_recv()
    matmul(3, 2)
    pair_copy(3).start()
    scatter(2)
    hits(1)
    scatter_last(3)
    scatter_sums(2)
    hits(2)
    reduce_rows(1)
    hits(3)
    add_owned(0)
    reduce_rows(2)
    reduce_rows(3)
    add_owned(1)
    add_owned(2)
    for k in range(CHUNKS):
        for delta in range(1, SRC):
            back_copy(k, delta).wait_recv()
    count_copy().wait_recv()
    seen_ref[...] = (counts[...] + pcounts[...]).T[:8]
    add_owned(3)

    flipped[...] = totals[...].T
    total_copy().start()
    total_copy().wait_recv()
    sums_ref[...] = flipped[at(core, 64), :] + ptotals[...]

    for delta in range(1, SRC):
        meta_copy(delta).wait_send()
    for delta in range(1, OWN):
        lab_copy(delta).wait_send()
    for k in range(CHUNKS):
        fwd_copy(k).wait_send()
        pair_copy(k).wait_send()
        for i in range(7):
            ag_copy(k, i).wait_send()
            rs_copy(k, i).wait_send()
        for delta in range(1, SRC):
            back_copy(k, delta).wait_send()
        for delta in range(1, OWN):
            dp_copy(k, delta).wait_send()
    count_copy().wait_send()
    total_copy().wait_send()


def per_device(points, landmarks, factor, assignments, owner_map, old_centroids):
    sharpness = math.sqrt(points.shape[1])
    vmem = pl.BlockSpec(memory_space=pltpu.VMEM)
    hbm = pl.BlockSpec(memory_space=pl.ANY)
    chunks = range(CHUNKS)
    sorted_features, perm, sums, seen = pl.pallas_call(
        functools.partial(body, sharpness),
        out_shape=(
            jax.ShapeDtypeStruct((PTS, RANK), BF16),
            jax.ShapeDtypeStruct((PTS, PTS), BF16),
            jax.ShapeDtypeStruct((64, KD), F32),
            jax.ShapeDtypeStruct((8, KD), F32),
        ),
        in_specs=[vmem, vmem, vmem, hbm, hbm],
        out_specs=(vmem, vmem, vmem, vmem),
        scratch_shapes=[
            pltpu.VMEM((LM, EMB), BF16),
            pltpu.VMEM((LM, RANK), BF16),
            pltpu.VMEM((8, 256), jnp.int32),
            pltpu.VMEM((SRC, 8, 256), jnp.int32),
            pltpu.VMEM((PTS, EMB), BF16),
            pltpu.VMEM((KD, COLS), F32),
            pltpu.VMEM((KD, COLS), F32),
            pltpu.VMEM((KD, COLS), F32),
            pltpu.VMEM((COLS, KD), F32),
            pltpu.VMEM((64, KD), F32),
            pltpu.VMEM((OWN, 1, CHUNKS * COLS), jnp.int32),
            pltpu.VMEM((OWN, 1, CHUNKS * COLS), jnp.int32),
            [pltpu.VMEM((2 * SRC * ROWS[k], EMB), BF16) for k in chunks],
            [pltpu.VMEM((2 * SRC * ROWS[k], RANK), F32) for k in chunks],
            [pltpu.VMEM((SRC * ROWS[k], RANK), F32) for k in chunks],
            [pltpu.VMEM((SRC, SRC * ROWS[k], COLS), BF16) for k in chunks],
            [pltpu.VMEM((SRC, SRC * ROWS[k], COLS), BF16) for k in chunks],
            [pltpu.VMEM((OWN * SRC * CAPS[k], SRC * ROWS[k]), BF16) for k in chunks],
            [pltpu.VMEM((KD, OWN * SRC * CAPS[k]), BF16) for k in chunks],
            [pltpu.VMEM((OWN * SRC * CAPS[k], COLS), BF16) for k in chunks],
            [pltpu.VMEM((OWN * SRC * CAPS[k], COLS), BF16) for k in chunks],
            pltpu.SemaphoreType.DMA((2,)),
            pltpu.SemaphoreType.DMA((2, SRC)),
            pltpu.SemaphoreType.DMA((2, CHUNKS, SRC)),
            pltpu.SemaphoreType.DMA((2, CHUNKS)),
            pltpu.SemaphoreType.DMA((2, CHUNKS)),
            pltpu.SemaphoreType.DMA((2, CHUNKS, SRC)),
            pltpu.SemaphoreType.DMA((2, CHUNKS, SRC)),
            pltpu.SemaphoreType.DMA((2, OWN)),
            pltpu.SemaphoreType.DMA((2, CHUNKS, OWN)),
            pltpu.SemaphoreType.DMA((2, 2)),
        ],
        name="nystrom",
        compiler_params=pltpu.CompilerParams(
            collective_id=1, has_side_effects=True, vmem_limit_bytes=60 * 2**20
        ),
    )(
        points,
        assignments.reshape(1, PTS),
        owner_map.reshape(128, 128),
        landmarks,
        factor,
    )
    features = lax.dot_general(
        perm, sorted_features, (((0,), (0,)), ((), ())), preferred_element_type=F32
    ).astype(BF16)
    seen = seen[0][:, None]
    centroids = jnp.where(seen > 0, sums.T / jnp.maximum(seen, 1.0), old_centroids)
    return (features, centroids)


def solution(mesh):
    in_specs = (
        P(("dp", "land"), None),
        P("land", None),
        P("land", None),
        P(("dp", "land")),
        P(),
        P("dp", "land"),
    )
    out_specs = (P(("dp", "land"), None), P("dp", "land"))
    return jax.shard_map(
        per_device, mesh=mesh, in_specs=in_specs, out_specs=out_specs, check_vma=False
    )
```
